32 devices in a mesh: seq: 8 (over y, x, core), exp: 4 (over z).
Axes of the slice: x: 2, y: 2, z: 4, core: 2. Of those that a mesh axis runs over, the one named last changes fastest.
Arguments:
- tokens: bfloat16 [1024, 2304], P('seq'), may hold values from -6 to 6
- norm_gain: bfloat16 [2304], replicated, may hold values from 0.099609375 to 1.8984375
- w_qkv: bfloat16 [2304, 3, 2048], P(None, None, 'exp'), may hold values from -12 to 12
- w_out: bfloat16 [2048, 2304], P('exp'), may hold values from -0.125 to 0.125
- moe_gain: bfloat16 [2304], replicated, may hold values from 0.099609375 to 1.8984375
- w_router: bfloat16 [2304, 4], replicated, may hold values from -0.25 to 0.25
- gate_up: bfloat16 [4, 2, 2304, 5760], P('exp', None, None, 'seq'), may hold values from -0.125 to 0.125
- w_down: bfloat16 [4, 5760, 2304], P('exp', 'seq'), may hold values from -0.078125 to 0.078125
- lengths: int32 [4], replicated, may hold values from 1 to 768, as said below
- blocks_seen: int32 [8, 8], P('seq'), may hold values from 0 to 1, as said below
- expert_ids: int32 [1024, 2], P(('seq', 'exp')), may hold values from 0 to 3, all different within a row; in each aligned block of 32 rows (0 to 31, 32 to 63, ...) at most 32 rows name the same one
- old_place: int32 [4], replicated, may hold values from 0 to 3, each once
- new_place: int32 [4], replicated, may hold values from 0 to 3, each once
Outputs:
- layer_out: bfloat16 [1024, 2304], P(('seq', 'exp'))
- new_gate_up: bfloat16 [4, 2, 2304, 5760], P('exp', None, None, 'seq')
- new_down: bfloat16 [4, 5760, 2304], P('exp', 'seq')
The draws below stay inside these ranges and needn't reach their ends.
Inputs may be any that keep to these rules, and one draw needn't show every extreme that they name: `lengths`: positive, summing to 1024, the largest exactly 768. `blocks_seen`: 1 on the diagonal; 0 above it and wherever no sequence has tokens in both blocks; elsewhere 0 or 1. `expert_ids`: the two experts of a token differ; among the 32 tokens of one device no expert is named more than 32 times, and in some devices one expert exactly 32 times. `old_place`: a permutation of the experts. `new_place`: a permutation of the experts.
All inputs are finite; a program needn't handle non-finite values.
Results may differ from the reference program's by a relative error of at most 0.023.
Values may be sent and summed in bfloat16 or wider, within the bound.
A program may use at most 128 MiB of HBM per device.

```python
import math
import jax
import jax.numpy as jnp
import numpy as np
from jax import lax

D = 2304
FF = 5760
HEAD_DIM = 64
TOP = 2
HEADS = 32
SEQS = 4
TOK_DEV = 128
EXPERTS = 4
TOKENS = 1024
BLOCKS = 8
TOK_SHARD = 32
MOST_LEN = 768
CAP = 32
N_SEQ = 8
N_EXP = 4


def doc_lengths(key):
    local_key = jax.random.fold_in(key, 7)
    first_key, second_key = jax.random.split(local_key)
    widths = jax.random.randint(first_key, (SEQS - 1,), 1000, 2001)
    spare = TOKENS - MOST_LEN - (SEQS - 1)
    running = jnp.cumsum(widths, dtype=jnp.int32)
    cuts = spare * running // running[-1]
    parts = 1 + jnp.diff(jnp.concatenate([jnp.zeros((1,), jnp.int32), cuts.astype(jnp.int32)]))
    whole = jnp.concatenate([jnp.full((1,), MOST_LEN, jnp.int32), parts.astype(jnp.int32)])
    offset = jax.random.randint(second_key, (), 0, SEQS)
    return jnp.roll(whole, offset)


def draw_lengths(key, part):
    return doc_lengths(key)


def draw_blocks_seen(key, part):
    seq_lengths = doc_lengths(key)
    ending = jnp.cumsum(seq_lengths, dtype=jnp.int32)
    block_range = jnp.arange(BLOCKS, dtype=jnp.int32)
    first_rows = block_range * TOK_DEV
    last_rows = first_rows + TOK_DEV - 1
    doc_first = jnp.sum((ending[None, :] <= first_rows[:, None]).astype(jnp.int32), axis=1)
    doc_last = jnp.sum((ending[None, :] <= last_rows[:, None]).astype(jnp.int32), axis=1)
    possible = (block_range[None, :] < block_range[:, None]) & (doc_last[None, :] == doc_first[:, None])
    keeping = jax.random.randint(jax.random.fold_in(key, 9), (BLOCKS, BLOCKS), 0, 3) == 0
    diagonal = block_range[:, None] == block_range[None, :]
    return (diagonal | possible & keeping).astype(jnp.int32)


def draw_tokens(key, part):
    first_key = jax.random.fold_in(jax.random.fold_in(key, 3), 0)
    drawn = jax.random.normal(first_key, (TOKENS, D), jnp.float32)
    return jnp.clip(drawn, -6.0, 6.0).astype(jnp.bfloat16)


def draw_w_qkv(key, part):
    columns = HEADS * HEAD_DIM
    drawn = jnp.clip(jax.random.normal(jax.random.fold_in(key, 5), (D, 3, columns), jnp.float32), -6.0, 6.0) / math.sqrt(D)
    return drawn.astype(jnp.bfloat16)


def block_scale(rng, shape, pieces, least, top_value):
    level, own = 1.0, jax.random.fold_in(rng, 6)
    for dim, blocks in pieces:
        heights = jnp.exp(jax.random.uniform(jax.random.fold_in(own, dim), (blocks,), jnp.float32, least / len(pieces), top_value / len(pieces)))
        level = level * jnp.repeat(heights, shape[dim] // blocks).reshape([-1 if axis == dim else 1 for axis in range(len(shape))])
    return level


def routed_block(own_key, own, number, rows, number_of, top, limit, lean):
    ranking = jax.random.permutation(own_key, number_of)
    packed, ordinary = portions_of(number_of, rows * top, limit, lean, True), portions_of(number_of, rows * top, limit, lean, False)
    places = jnp.arange(number_of)

    def named(sizes, turn):
        used = int((sizes > 0).sum())
        fixed = max(1, used // 4)
        shifted = fixed + (places - fixed + turn * (used - fixed)) % max(1, number_of - fixed)
        return jnp.zeros((number_of,), jnp.int32).at[ranking[jnp.where(places < fixed, places, shifted)]].set(jnp.asarray(sizes, jnp.int32))

    sizes = jnp.where(number % 4 == 0, named(packed, number // 4), named(ordinary, number - number // 4 - 1))
    mixed = jax.random.permutation(jax.random.fold_in(own, 3), number_of)
    giver, receiver = mixed[0:number_of // 2 * 2:2], mixed[1:number_of // 2 * 2:2]
    slack = jnp.minimum(sizes[giver] - 1, limit - sizes[receiver]) // 2
    slack = jnp.where((giver == ranking[0]) | (receiver == ranking[0]) | (sizes[receiver] == 0), 0, jnp.maximum(slack, 0))
    shifted = jax.random.randint(jax.random.fold_in(own, 4), (number_of // 2,), 0, 1 << 20) % (slack + 1)
    sizes = sizes.at[giver].add(-shifted).at[receiver].add(shifted)
    labels = jnp.searchsorted(jnp.cumsum(sizes), jnp.arange(rows * top), side="right").astype(jnp.int32)
    grid = labels.reshape(top, rows).T
    grid = grid[jax.random.permutation(jax.random.fold_in(own, 1), rows)]
    turn = jax.random.randint(jax.random.fold_in(own, 2), (rows, 1), 0, top)
    return jnp.take_along_axis(grid, (jnp.arange(top)[None, :] + turn) % top, axis=1)


def portions_of(count, total, bound, slope, full):
    loads = [(1 << 20) // math.isqrt(grade ** slope) + 1 for grade in range(1, count + 1)]
    largest = bound if full else min(bound, max(-(-total // count), total * loads[0] // sum(loads)))
    least = 1 if total - largest >= count - 1 else 0
    counts, rest = [largest] + [least] * (count - 1), total - largest - least * (count - 1)
    while rest > 0:
        free = [i for i in range(1, count) if counts[i] < largest] or [i for i in range(1, count) if counts[i] < bound]
        pool, left = sum([loads[i] for i in free]), rest
        for i in free:
            addition = min(bound - counts[i], max(1, left * loads[i] // pool), rest)
            counts[i] = counts[i] + addition
            rest = rest - addition
    return np.array(counts)


def bell_draw(key, dims, deviation, bound, pieces=(), kind=jnp.bfloat16):
    factor_of = block_scale(key, dims, pieces, -0.22, 0.18) if pieces else 1.0
    values = jax.random.normal(key, dims, jnp.float32) * deviation * factor_of
    return jnp.minimum(jnp.maximum(values, -bound), bound).astype(kind)


def setup_inputs(seed: int = 0) -> dict:
    splits = jax.random.split(jax.random.key(seed), 14)
    tokens = draw_tokens(jax.random.fold_in(splits[13], 71), 0)
    norm_gain = jnp.clip(1.0 + 0.18 * jax.random.normal(splits[1], (D,), jnp.float32), 0.099609375, 1.8984375).astype(jnp.bfloat16)
    w_qkv = draw_w_qkv(jax.random.fold_in(splits[13], 71), 0)
    w_out = bell_draw(splits[3], (HEADS * HEAD_DIM, D), (HEADS * HEAD_DIM) ** -0.5, 0.125, ((0, 4),))
    moe_gain = jnp.clip(1.0 + 0.18 * jax.random.normal(splits[4], (D,), jnp.float32), 0.099609375, 1.8984375).astype(jnp.bfloat16)
    w_router = bell_draw(splits[5], (D, EXPERTS), (D // 4) ** -0.5, 0.25)
    gate_up = bell_draw(splits[6], (EXPERTS, 2, D, FF), D ** -0.5, 0.125, ((0, 4), (3, 8)))
    w_down = bell_draw(splits[7], (EXPERTS, FF, D), FF ** -0.5, 0.078125, ((0, 4), (1, 8)))
    lengths = draw_lengths(jax.random.fold_in(splits[13], 71), 0)
    blocks_seen = draw_blocks_seen(jax.random.fold_in(splits[13], 71), 0)
    expert_ids_keys = jax.random.split(jax.random.fold_in(splits[10], 1), TOKENS // TOK_SHARD)
    expert_ids_turns = jax.random.permutation(jax.random.fold_in(splits[10], 3), TOKENS // TOK_SHARD)
    expert_ids = jax.vmap(lambda own, number: routed_block(jax.random.fold_in(splits[10], 2), own, number, TOK_SHARD, EXPERTS, TOP, CAP, 2))(expert_ids_keys, expert_ids_turns).reshape((TOKENS, TOP))
    old_place = jax.random.permutation(splits[11], EXPERTS).astype(jnp.int32)
    new_place = jax.random.permutation(splits[12], EXPERTS).astype(jnp.int32)
    return {"tokens": tokens, "norm_gain": norm_gain, "w_qkv": w_qkv, "w_out": w_out, "moe_gain": moe_gain, "w_router": w_router, "gate_up": gate_up, "w_down": w_down, "lengths": lengths, "blocks_seen": blocks_seen, "expert_ids": expert_ids, "old_place": old_place, "new_place": new_place}


epsilon = 1e-05
masked_score = -1e+30

def rms_scale(values_in, gain):
    widened = values_in.astype(jnp.float32)
    inverse = lax.rsqrt(lax.optimization_barrier(jnp.mean(widened * widened, axis=-1, keepdims=True)) + epsilon)
    return widened * inverse * gain.astype(jnp.float32)

def rotate(vectors, angle_base):
    halfway = vectors.shape[-1] // 2
    spacing = jnp.arange(halfway, dtype=jnp.float32) / halfway
    freqs_all = jnp.exp(-jnp.log(10000.0) * spacing)
    angles = angle_base[:, None] * freqs_all[None, :]
    cosine = jnp.cos(angles)[:, None, :]
    sine_part = jnp.sin(angles)[:, None, :]
    leading = vectors[..., :halfway]
    trailing = vectors[..., halfway:]
    return jnp.concatenate([leading * cosine - trailing * sine_part, trailing * cosine + leading * sine_part], axis=-1)

def doc_layout(seq_lengths, row_ids):
    ending = jnp.cumsum(seq_lengths, dtype=jnp.int32)
    passed = (ending[None, :] <= row_ids[:, None]).astype(jnp.int32)
    doc_ids = lax.optimization_barrier(jnp.sum(passed, axis=1, dtype=jnp.int32))
    starting = lax.optimization_barrier(jnp.sum(passed * seq_lengths[None, :], axis=1, dtype=jnp.int32))
    return (doc_ids, row_ids - starting)

def reference(tokens, norm_gain, w_qkv, w_out, moe_gain, w_router, gate_up, w_down, lengths, blocks_seen, expert_ids, old_place, new_place):
    row_ids = jnp.arange(TOKENS, dtype=jnp.int32)
    doc_ids, places = doc_layout(lengths, row_ids)
    normed = rms_scale(tokens, norm_gain).astype(jnp.bfloat16)
    projected = jnp.dot(normed, w_qkv.reshape(D, 3 * HEADS * HEAD_DIM), preferred_element_type=jnp.float32)
    projected = projected.reshape(TOKENS, 3, HEADS, HEAD_DIM)
    angle_rows = places.astype(jnp.float32)
    queries = rotate(projected[:, 0], angle_rows).astype(jnp.bfloat16)
    key_all = rotate(projected[:, 1], angle_rows).astype(jnp.bfloat16)
    value_all = projected[:, 2].astype(jnp.bfloat16)
    block_ids = row_ids // TOK_DEV
    allowed = (doc_ids[:, None] == doc_ids[None, :]) & (row_ids[None, :] <= row_ids[:, None]) & (blocks_seen[block_ids[:, None], block_ids[None, :]] == 1)
    score_scale = HEAD_DIM ** (-0.5)

    def one_head(operands):
        query_head, key_head, value_head = operands
        scores = jnp.dot(query_head, key_head.T, preferred_element_type=jnp.float32) * score_scale
        scores = jnp.where(allowed, scores, masked_score)
        largest = lax.optimization_barrier(jnp.max(scores, axis=1, keepdims=True))
        weights = jnp.where(allowed, jnp.exp(scores - largest), 0.0)
        totals = lax.optimization_barrier(jnp.sum(weights, axis=1, keepdims=True))
        mixed_rows = jnp.dot(weights.astype(jnp.bfloat16), value_head, preferred_element_type=jnp.float32)
        return (mixed_rows / totals).astype(jnp.bfloat16)
    attended = lax.map(one_head, (jnp.swapaxes(queries, 0, 1), jnp.swapaxes(key_all, 0, 1), jnp.swapaxes(value_all, 0, 1)))
    attended = jnp.swapaxes(attended, 0, 1).reshape(TOKENS, HEADS * HEAD_DIM)
    hidden = (tokens.astype(jnp.float32) + jnp.dot(attended, w_out, preferred_element_type=jnp.float32)).astype(jnp.bfloat16)
    moe_in = rms_scale(hidden, moe_gain).astype(jnp.bfloat16)
    logits = jnp.dot(moe_in, w_router, preferred_element_type=jnp.float32)
    expert_range = jnp.arange(EXPERTS, dtype=jnp.int32)
    chosen = lax.optimization_barrier(jnp.sum(jnp.where(expert_ids[:, :, None] == expert_range[None, None, :], logits[:, None, :], 0.0), axis=2))
    gate_first = 1.0 / (1.0 + jnp.exp(chosen[:, 1] - chosen[:, 0]))
    gate_second = 1.0 / (1.0 + jnp.exp(chosen[:, 0] - chosen[:, 1]))
    gating = jnp.stack([gate_first, gate_second], axis=1)
    slot_of = lax.optimization_barrier(jnp.sum(jnp.where(old_place[:, None] == expert_range[None, :], expert_range[:, None], 0), axis=0, dtype=jnp.int32))
    slice_width = FF // N_SEQ
    capacity_rows = min(TOKENS, N_SEQ * N_EXP * CAP)

    def add_expert(moe_sum, expert):
        routed = jnp.any(expert_ids == expert, axis=1)
        found_rows = jnp.nonzero(routed, size=capacity_rows, fill_value=0)[0].astype(jnp.int32)
        valid_rows = jnp.arange(capacity_rows, dtype=jnp.int32) < jnp.sum(routed.astype(jnp.int32), dtype=jnp.int32)
        inputs = moe_in[found_rows]
        slot_index = slot_of[expert]
        gate_slices = jnp.moveaxis(gate_up[slot_index].reshape(2, D, N_SEQ, slice_width), 2, 0)
        down_slices = w_down[slot_index].reshape(N_SEQ, slice_width, D)

        def add_slice(running, operands):
            pair_weights, down_weights = operands
            gate_part = jnp.dot(inputs, pair_weights[0], preferred_element_type=jnp.float32)
            up_part = jnp.dot(inputs, pair_weights[1], preferred_element_type=jnp.float32)
            activated = (jax.nn.silu(gate_part) * up_part).astype(jnp.bfloat16)
            slice_term = jnp.dot(activated, down_weights, preferred_element_type=jnp.float32).astype(jnp.bfloat16)
            slice_term = lax.optimization_barrier(slice_term)
            return (running + slice_term.astype(jnp.float32), None)
        summed, _ = lax.scan(add_slice, jnp.zeros((capacity_rows, D), jnp.float32), (gate_slices, down_slices))
        expert_out = lax.optimization_barrier(summed.astype(jnp.bfloat16)).astype(jnp.float32)
        chosen_gate = lax.optimization_barrier(jnp.sum(jnp.where(expert_ids[found_rows] == expert, gating[found_rows], 0.0), axis=1))
        weighted = jnp.where(valid_rows[:, None], chosen_gate[:, None] * expert_out, 0.0)
        return (moe_sum.at[found_rows].add(weighted), None)
    moe_sum, _ = lax.scan(add_expert, jnp.zeros((TOKENS, D), jnp.float32), expert_range)
    layer_out = (hidden.astype(jnp.float32) + moe_sum).astype(jnp.bfloat16)
    source_slot = lax.optimization_barrier(jnp.sum(jnp.where(new_place[:, None] == expert_range[None, :], slot_of[None, :], 0), axis=1, dtype=jnp.int32))
    new_gate_up = gate_up[source_slot]
    new_down = w_down[source_slot]
    return (layer_out, new_gate_up, new_down)
```

```python
import jax
import jax.numpy as jnp
from jax import lax
from jax.sharding import PartitionSpec as P

HEAD_DIM = 64


epsilon = 1e-05
masked_score = -1e30


def rms_scale(values_in, gain):
    widened = values_in.astype(jnp.float32)
    inverse = lax.rsqrt(jnp.mean(widened * widened, axis=-1, keepdims=True) + epsilon)
    return widened * inverse * gain.astype(jnp.float32)


def rotate(vectors, angle_base):
    halfway = vectors.shape[-1] // 2
    spacing = jnp.arange(halfway, dtype=jnp.float32) / halfway
    freqs_all = jnp.exp(-jnp.log(10000.0) * spacing)
    angles = angle_base[:, None] * freqs_all[None, :]
    cosine = jnp.cos(angles)[:, None, :]
    sine_part = jnp.sin(angles)[:, None, :]
    leading = vectors[..., :halfway]
    trailing = vectors[..., halfway:]
    return jnp.concatenate(
        [leading * cosine - trailing * sine_part, trailing * cosine + leading * sine_part], axis=-1
    )


def doc_layout(seq_lengths, row_ids):
    ending = jnp.cumsum(seq_lengths, dtype=jnp.int32)
    passed = (ending[None, :] <= row_ids[:, None]).astype(jnp.int32)
    doc_ids = jnp.sum(passed, axis=1, dtype=jnp.int32)
    starting = jnp.sum(passed * seq_lengths[None, :], axis=1, dtype=jnp.int32)
    return (doc_ids, row_ids - starting)


def owner_table(placing):
    slot_range = jnp.arange(placing.shape[0], dtype=jnp.int32)
    return jnp.sum(
        jnp.where(placing[:, None] == slot_range[None, :], slot_range[:, None], 0),
        axis=0,
        dtype=jnp.int32,
    )


def attend(queries, key_all, value_all, allowed):
    score_scale = queries.shape[-1] ** (-0.5)
    scores = (
        jnp.einsum("qhd,khd->hqk", queries, key_all, preferred_element_type=jnp.float32)
        * score_scale
    )
    scores = jnp.where(allowed[None], scores, masked_score)
    largest = jnp.max(scores, axis=2, keepdims=True)
    weights = jnp.where(allowed[None], jnp.exp(scores - largest), 0.0)
    totals = jnp.sum(weights, axis=2)
    summed = jnp.einsum(
        "hqk,khd->hqd",
        weights.astype(jnp.bfloat16),
        value_all,
        preferred_element_type=jnp.float32,
    )
    return (summed / totals[:, :, None]).astype(jnp.bfloat16)


def from_xor(value, distance):
    count = lax.axis_size("seq")
    return lax.ppermute(value, "seq", [(i, i ^ distance) for i in range(count)])


def gather_xor(value):
    count = lax.axis_size("seq")
    even = [value] + [from_xor(value, k) for k in range(2, count, 2)]
    even = jnp.stack(even)
    odd = from_xor(even, 1)
    return jnp.stack([even, odd], axis=1).reshape((count,) + value.shape)


def reduce_xor(parts):
    count = lax.axis_size("seq")
    pairs = parts.reshape((count // 2, 2) + parts.shape[1:])
    got = from_xor(pairs[:, 1], 1)
    both = pairs[:, 0].astype(jnp.float32) + got.astype(jnp.float32)
    total = both[0]
    sent = both[1:].astype(jnp.bfloat16)
    for k in range(1, count // 2):
        total = total + from_xor(sent[k - 1], 2 * k).astype(jnp.float32)
    return total


def move_by_exchange(gate_up, w_down, source_slot):
    slot_index = lax.axis_index("exp")
    slots = lax.axis_size("exp")
    steps = 9
    slot_range = jnp.arange(slots, dtype=jnp.int32)
    dest = owner_table(source_slot)
    crossed = (dest[0] >= 2) & (dest[1] >= 2)
    swapped = jnp.array([0, 2, 1, 3], jnp.int32)
    middle = jnp.where(crossed, swapped, slot_range)
    source_first = jnp.sum(
        jnp.where(middle[:, None] == slot_range[None, :], source_slot[None, :], 0), axis=1
    )
    dest_first = owner_table(source_first)
    own_dest = jnp.sum(jnp.where(slot_range == slot_index, dest_first, 0))
    own_source = jnp.sum(jnp.where(slot_range == slot_index, source_first, 0))
    gate_rows = jnp.swapaxes(gate_up, 2, 3)
    gate = gate_rows.reshape(2, steps, gate_rows.shape[2] // steps, gate_rows.shape[3])
    down = w_down.reshape(steps, w_down.shape[1] // steps, w_down.shape[2])
    gate_new, down_new = gate, down
    upward = [(i, i + 1) for i in range(slots - 1)]
    downward = [(i + 1, i) for i in range(slots - 1)]
    above = slots - 1 - slot_index
    use_up = own_source < slot_index
    moved = own_source != slot_index
    gate_got = down_got = None

    def pick(gate_part, down_part, at):
        at = jnp.clip(at, 0, steps - 1)
        return (
            lax.dynamic_index_in_dim(gate_part, at, 1, keepdims=False),
            lax.dynamic_index_in_dim(down_part, at, 0, keepdims=False),
        )

    got_up = got_down = None
    for step in range(steps + slots - 2):
        up = pick(gate, down, step - slot_index)
        low = pick(gate, down, step - above)
        if got_up is not None:
            up = tuple(jnp.where(own_dest > slot_index, a, b) for a, b in zip(up, got_up))
            low = tuple(jnp.where(own_dest < slot_index, a, b) for a, b in zip(low, got_down))
        got_up = tuple(lax.ppermute(a, "exp", upward) for a in up)
        got_down = tuple(lax.ppermute(a, "exp", downward) for a in low)
        at = jnp.where(use_up, step - slot_index + 1, step - above + 1)
        keep = moved & (at >= 0) & (at < steps)
        at = jnp.clip(at, 0, steps - 1)
        old = pick(gate_new, down_new, at)
        fresh = tuple(
            jnp.where(keep, jnp.where(use_up, a, b), c)
            for a, b, c in zip(got_up, got_down, old)
        )
        gate_new = lax.dynamic_update_index_in_dim(gate_new, fresh[0], at, 1)
        down_new = lax.dynamic_update_index_in_dim(down_new, fresh[1], at, 0)

    def swap_middle(held):
        other = [lax.ppermute(a, "exp", [(1, 2), (2, 1)]) for a in held]
        inner = (slot_index == 1) | (slot_index == 2)
        return tuple(jnp.where(inner, a, b) for a, b in zip(other, held))

    gate_new, down_new = lax.cond(crossed, swap_middle, lambda held: held, (gate_new, down_new))
    gate_new = jnp.swapaxes(gate_new.reshape(gate_rows.shape), 2, 3)
    return gate_new, down_new.reshape(w_down.shape)


def move_by_scatter(gate_up, w_down, source_slot):
    exp_count = lax.axis_size("exp")
    model_width, slice_width = gate_up.shape[2:]
    piece_width = model_width // exp_count
    gate_split = gate_up.reshape(2, exp_count, piece_width, slice_width)
    down_split = w_down.reshape(slice_width, exp_count, piece_width)
    gate_held = lax.all_to_all(gate_split, "exp", split_axis=1, concat_axis=1, tiled=True)
    down_held = lax.all_to_all(down_split, "exp", split_axis=1, concat_axis=1, tiled=True)
    gate_sorted = jnp.take(gate_held, source_slot, axis=1)
    down_sorted = jnp.take(down_held, source_slot, axis=1)
    gate_moved = lax.all_to_all(gate_sorted, "exp", split_axis=1, concat_axis=1, tiled=True)
    down_moved = lax.all_to_all(down_sorted, "exp", split_axis=1, concat_axis=1, tiled=True)
    return gate_moved.reshape(gate_up.shape), down_moved.reshape(w_down.shape)


def shards(
    tokens,
    norm_gain,
    w_qkv,
    w_out,
    moe_gain,
    w_router,
    gate_up,
    w_down,
    lengths,
    blocks_seen,
    expert_ids,
    old_place,
    new_place,
):
    block_rows = tokens.shape[0]
    model_width = tokens.shape[1]
    exp_count = lax.axis_size("exp")
    seq_count = lax.axis_size("seq")
    block_index = lax.axis_index("seq")
    slot_index = lax.axis_index("exp")
    expert_range = jnp.arange(w_router.shape[1], dtype=jnp.int32)

    slot_old = owner_table(old_place)
    source_slot = jnp.sum(
        jnp.where(new_place[:, None] == expert_range[None, :], slot_old[None, :], 0),
        axis=1,
        dtype=jnp.int32,
    )
    movable = exp_count == 4 and w_down.shape[1] % 9 == 0
    move = move_by_exchange if movable else move_by_scatter
    new_gate_up, new_down = move(gate_up, w_down, source_slot)

    ids_all = lax.all_gather(expert_ids, ("seq", "exp"), axis=0, tiled=True)
    heads_here = w_qkv.shape[2] // HEAD_DIM
    query_rows = block_index * block_rows + jnp.arange(block_rows, dtype=jnp.int32)
    query_docs, query_places = doc_layout(lengths, query_rows)
    normed = rms_scale(tokens, norm_gain).astype(jnp.bfloat16)
    projected = [
        jnp.dot(normed, w_qkv[:, part], preferred_element_type=jnp.float32).reshape(
            block_rows, heads_here, HEAD_DIM
        )
        for part in range(3)
    ]
    angle_rows = query_places.astype(jnp.float32)
    queries = rotate(projected[0], angle_rows).astype(jnp.bfloat16)
    key_block = rotate(projected[1], angle_rows).astype(jnp.bfloat16)
    value_block = projected[2].astype(jnp.bfloat16)
    pair = jnp.concatenate(
        [key_block.reshape(block_rows, -1), value_block.reshape(block_rows, -1)], axis=1
    )
    pair_all = gather_xor(pair).reshape(seq_count * block_rows, 2, heads_here, HEAD_DIM)
    order = block_index ^ jnp.arange(seq_count, dtype=jnp.int32)
    key_rows = (
        order[:, None] * block_rows + jnp.arange(block_rows, dtype=jnp.int32)[None, :]
    ).reshape(-1)
    key_docs, _ = doc_layout(lengths, key_rows)
    seen = jnp.take(blocks_seen[0], order)
    key_seen = jnp.repeat(seen, block_rows) == 1
    allowed = (
        (query_docs[:, None] == key_docs[None, :])
        & (key_rows[None, :] <= query_rows[:, None])
        & key_seen[None, :]
    )
    attended = attend(queries, pair_all[:, 0], pair_all[:, 1], allowed)
    attended = jnp.transpose(attended, (1, 0, 2)).reshape(block_rows, heads_here * HEAD_DIM)
    shard_rows = block_rows // exp_count
    partial = jnp.dot(attended, w_out, preferred_element_type=jnp.float32).astype(jnp.bfloat16)
    partials = lax.all_to_all(
        partial.reshape(exp_count, shard_rows, model_width), "exp", 0, 0, tiled=True
    )
    head_total = jnp.sum(partials.astype(jnp.float32), axis=0)
    residual = lax.dynamic_slice_in_dim(tokens, slot_index * shard_rows, shard_rows, 0)
    hidden = (residual.astype(jnp.float32) + head_total).astype(jnp.bfloat16)
    moe_in = rms_scale(hidden, moe_gain).astype(jnp.bfloat16)
    spread = jnp.broadcast_to(moe_in[None], (exp_count,) + moe_in.shape)
    block_in = lax.all_to_all(spread, "exp", 0, 0, tiled=True)
    flat_rows = gather_xor(block_in.reshape(block_rows, model_width)).reshape(-1, model_width)

    ids = jnp.take(ids_all.reshape(seq_count, block_rows, 2), order, axis=0).reshape(-1, 2)
    logits = jnp.dot(flat_rows, w_router, preferred_element_type=jnp.float32)
    chosen = jnp.sum(
        jnp.where(ids[:, :, None] == expert_range[None, None, :], logits[:, None, :], 0.0),
        axis=2,
    )
    gate_first = 1.0 / (1.0 + jnp.exp(chosen[:, 1] - chosen[:, 0]))
    gate_second = 1.0 / (1.0 + jnp.exp(chosen[:, 0] - chosen[:, 1]))
    here = jnp.sum(jnp.where(expert_range == slot_index, old_place, 0))
    gating = jnp.where(
        ids[:, 0] == here, gate_first, jnp.where(ids[:, 1] == here, gate_second, 0.0)
    )
    projected_gate = jnp.dot(flat_rows, gate_up[0, 0], preferred_element_type=jnp.float32)
    projected_up = jnp.dot(flat_rows, gate_up[0, 1], preferred_element_type=jnp.float32)
    activated = (jax.nn.silu(projected_gate) * projected_up).astype(jnp.bfloat16)
    flat_out = jnp.dot(activated, w_down[0], preferred_element_type=jnp.float32)
    weighted = (flat_out * gating[:, None]).astype(jnp.bfloat16)
    summed = reduce_xor(weighted.reshape(seq_count, block_rows, model_width))
    returned = lax.all_to_all(
        summed.astype(jnp.bfloat16).reshape(exp_count, shard_rows, model_width),
        "exp",
        0,
        0,
        tiled=True,
    )
    moe_sum = jnp.sum(returned.astype(jnp.float32), axis=0)
    layer_out = (hidden.astype(jnp.float32) + moe_sum).astype(jnp.bfloat16)
    return (layer_out, new_gate_up, new_down)


def solution(mesh):
    in_specs = (
        P("seq", None),
        P(),
        P(None, None, "exp"),
        P("exp", None),
        P(),
        P(),
        P("exp", None, None, "seq"),
        P("exp", "seq", None),
        P(),
        P("seq", None),
        P(("seq", "exp"), None),
        P(),
        P(),
    )
    out_specs = (P(("seq", "exp"), None), P("exp", None, None, "seq"), P("exp", "seq", None))
    return jax.shard_map(shards, mesh=mesh, in_specs=in_specs, out_specs=out_specs, check_vma=False)
```

```python
import itertools

import jax
import jax.numpy as jnp
import numpy as np
from jax import lax
from jax.sharding import PartitionSpec as P

HEAD_DIM = 64


epsilon = 1e-05
masked_score = -1e30


def rms_scale(values_in, gain):
    widened = values_in.astype(jnp.float32)
    inverse = lax.rsqrt(jnp.mean(widened * widened, axis=-1, keepdims=True) + epsilon)
    return widened * inverse * gain.astype(jnp.float32)


def rotate(vectors, angle_base):
    halfway = vectors.shape[-1] // 2
    spacing = jnp.arange(halfway, dtype=jnp.float32) / halfway
    freqs_all = jnp.exp(-jnp.log(10000.0) * spacing)
    angles = angle_base[:, None] * freqs_all[None, :]
    cosine = jnp.cos(angles)[:, None, :]
    sine_part = jnp.sin(angles)[:, None, :]
    leading = vectors[..., :halfway]
    trailing = vectors[..., halfway:]
    return jnp.concatenate(
        [leading * cosine - trailing * sine_part, trailing * cosine + leading * sine_part], axis=-1
    )


def doc_layout(seq_lengths, row_ids):
    ending = jnp.cumsum(seq_lengths, dtype=jnp.int32)
    passed = (ending[None, :] <= row_ids[:, None]).astype(jnp.int32)
    doc_ids = jnp.sum(passed, axis=1, dtype=jnp.int32)
    starting = jnp.sum(passed * seq_lengths[None, :], axis=1, dtype=jnp.int32)
    return (doc_ids, row_ids - starting)


def owner_table(placing):
    slot_range = jnp.arange(placing.shape[0], dtype=jnp.int32)
    return jnp.sum(
        jnp.where(placing[:, None] == slot_range[None, :], slot_range[:, None], 0),
        axis=0,
        dtype=jnp.int32,
    )


def attend(queries, key_all, value_all, allowed):
    score_scale = queries.shape[-1] ** (-0.5)
    scores = (
        jnp.einsum("qhd,khd->hqk", queries, key_all, preferred_element_type=jnp.float32)
        * score_scale
    )
    scores = jnp.where(allowed[None], scores, masked_score)
    largest = jnp.max(scores, axis=2, keepdims=True)
    weights = jnp.where(allowed[None], jnp.exp(scores - largest), 0.0)
    totals = jnp.sum(weights, axis=2)
    summed = jnp.einsum(
        "hqk,khd->hqd",
        weights.astype(jnp.bfloat16),
        value_all,
        preferred_element_type=jnp.float32,
    )
    return (summed / totals[:, :, None]).astype(jnp.bfloat16)


def from_xor(value, distance):
    count = lax.axis_size("seq")
    return lax.ppermute(value, "seq", [(i, i ^ distance) for i in range(count)])


def gather_xor(value):
    count = lax.axis_size("seq")
    even = [value] + [from_xor(value, k) for k in range(2, count, 2)]
    even = jnp.stack(even)
    odd = from_xor(even, 1)
    return jnp.stack([even, odd], axis=1).reshape((count,) + value.shape)


def reduce_xor(parts):
    count = lax.axis_size("seq")
    pairs = parts.reshape((count // 2, 2) + parts.shape[1:])
    got = from_xor(pairs[:, 1], 1)
    both = pairs[:, 0].astype(jnp.float32) + got.astype(jnp.float32)
    total = both[0]
    sent = both[1:].astype(jnp.bfloat16)
    for k in range(1, count // 2):
        total = total + from_xor(sent[k - 1], 2 * k).astype(jnp.float32)
    return total


def move_by_scatter(gate_up, w_down, source_slot):
    exp_count = lax.axis_size("exp")
    model_width, slice_width = gate_up.shape[2:]
    piece_width = model_width // exp_count
    gate_split = gate_up.reshape(2, exp_count, piece_width, slice_width)
    down_split = w_down.reshape(slice_width, exp_count, piece_width)
    gate_held = lax.all_to_all(gate_split, "exp", split_axis=1, concat_axis=1, tiled=True)
    down_held = lax.all_to_all(down_split, "exp", split_axis=1, concat_axis=1, tiled=True)
    gate_sorted = jnp.take(gate_held, source_slot, axis=1)
    down_sorted = jnp.take(down_held, source_slot, axis=1)
    gate_moved = lax.all_to_all(gate_sorted, "exp", split_axis=1, concat_axis=1, tiled=True)
    down_moved = lax.all_to_all(down_sorted, "exp", split_axis=1, concat_axis=1, tiled=True)
    return gate_moved.reshape(gate_up.shape), down_moved.reshape(w_down.shape)


def prepare(tokens, norm_gain, w_qkv, lengths, blocks_seen):
    block_rows = tokens.shape[0]
    seq_count = lax.axis_size("seq")
    block_index = lax.axis_index("seq")
    heads_here = w_qkv.shape[2] // HEAD_DIM
    query_rows = block_index * block_rows + jnp.arange(block_rows, dtype=jnp.int32)
    query_docs, query_places = doc_layout(lengths, query_rows)
    normed = rms_scale(tokens, norm_gain).astype(jnp.bfloat16)
    projected = [
        jnp.dot(normed, w_qkv[:, part], preferred_element_type=jnp.float32).reshape(
            block_rows, heads_here, HEAD_DIM
        )
        for part in range(3)
    ]
    angle_rows = query_places.astype(jnp.float32)
    queries = rotate(projected[0], angle_rows).astype(jnp.bfloat16)
    key_block = rotate(projected[1], angle_rows).astype(jnp.bfloat16)
    value_block = projected[2].astype(jnp.bfloat16)
    pair = jnp.concatenate(
        [key_block.reshape(block_rows, -1), value_block.reshape(block_rows, -1)], axis=1
    )
    order = block_index ^ jnp.arange(seq_count, dtype=jnp.int32)
    key_rows = (
        order[:, None] * block_rows + jnp.arange(block_rows, dtype=jnp.int32)[None, :]
    ).reshape(-1)
    key_docs, _ = doc_layout(lengths, key_rows)
    seen = jnp.take(blocks_seen[0], order)
    key_seen = jnp.repeat(seen, block_rows) == 1
    allowed = (
        (query_docs[:, None] == key_docs[None, :])
        & (key_rows[None, :] <= query_rows[:, None])
        & key_seen[None, :]
    )
    return queries, pair, allowed


def layer(
    queries,
    pair,
    allowed,
    tokens,
    w_out,
    moe_gain,
    w_router,
    gate_up,
    w_down,
    expert_ids,
    old_place,
    moving=(),
):
    block_rows = tokens.shape[0]
    model_width = tokens.shape[1]
    exp_count = lax.axis_size("exp")
    moving = list(moving)
    seq_count = lax.axis_size("seq")
    slot_index = lax.axis_index("exp")
    expert_range = jnp.arange(w_router.shape[1], dtype=jnp.int32)
    heads_here = queries.shape[1]
    pair_all = gather_xor(pair).reshape(seq_count * block_rows, 2, heads_here, HEAD_DIM)
    attended = attend(queries, pair_all[:, 0], pair_all[:, 1], allowed)
    attended = jnp.transpose(attended, (1, 0, 2)).reshape(block_rows, heads_here * HEAD_DIM)
    shard_rows = block_rows // exp_count
    partial = jnp.dot(attended, w_out, preferred_element_type=jnp.float32).astype(jnp.bfloat16)
    partials = lax.all_to_all(
        partial.reshape(exp_count, shard_rows, model_width), "exp", 0, 0, tiled=True
    )
    head_total = jnp.sum(partials.astype(jnp.float32), axis=0)
    residual = lax.dynamic_slice_in_dim(tokens, slot_index * shard_rows, shard_rows, 0)
    hidden = (residual.astype(jnp.float32) + head_total).astype(jnp.bfloat16)
    moe_in = rms_scale(hidden, moe_gain).astype(jnp.bfloat16)
    named = jnp.pad(expert_ids.astype(jnp.bfloat16), ((0, 0), (0, 126)))
    labelled = jnp.concatenate([moe_in, named], axis=1)
    spread = jnp.broadcast_to(labelled[None], (exp_count,) + labelled.shape)
    block_in = lax.all_to_all(spread, "exp", 0, 0, tiled=True).reshape(block_rows, -1)
    if moving:
        block_in, moving[0] = lax.optimization_barrier((block_in, moving[0]))
    all_rows = gather_xor(block_in).reshape(seq_count * block_rows, -1)
    flat_rows = all_rows[:, :model_width]
    ids = all_rows[:, model_width : model_width + 2].astype(jnp.int32)
    logits = jnp.dot(flat_rows, w_router, preferred_element_type=jnp.float32)
    chosen = jnp.sum(
        jnp.where(ids[:, :, None] == expert_range[None, None, :], logits[:, None, :], 0.0),
        axis=2,
    )
    gate_first = 1.0 / (1.0 + jnp.exp(chosen[:, 1] - chosen[:, 0]))
    gate_second = 1.0 / (1.0 + jnp.exp(chosen[:, 0] - chosen[:, 1]))
    here = jnp.sum(jnp.where(expert_range == slot_index, old_place, 0))
    gating = jnp.where(
        ids[:, 0] == here, gate_first, jnp.where(ids[:, 1] == here, gate_second, 0.0)
    )
    projected_gate = jnp.dot(flat_rows, gate_up[0, 0], preferred_element_type=jnp.float32)
    projected_up = jnp.dot(flat_rows, gate_up[0, 1], preferred_element_type=jnp.float32)
    activated = (jax.nn.silu(projected_gate) * projected_up).astype(jnp.bfloat16)
    flat_out = jnp.dot(activated, w_down[0], preferred_element_type=jnp.float32)
    weighted = (flat_out * gating[:, None]).astype(jnp.bfloat16)
    if moving:
        weighted, moving[1] = lax.optimization_barrier((weighted, moving[1]))
    summed = reduce_xor(weighted.reshape(seq_count, block_rows, model_width))
    returned = lax.all_to_all(
        summed.astype(jnp.bfloat16).reshape(exp_count, shard_rows, model_width),
        "exp",
        0,
        0,
        tiled=True,
    )
    moe_sum = jnp.sum(returned.astype(jnp.float32), axis=0)
    layer_out = (hidden.astype(jnp.float32) + moe_sum).astype(jnp.bfloat16)
    return layer_out, moving


def shards(
    tokens,
    norm_gain,
    w_qkv,
    w_out,
    moe_gain,
    w_router,
    gate_up,
    w_down,
    lengths,
    blocks_seen,
    expert_ids,
    old_place,
    new_place,
):
    slots = lax.axis_size("exp")
    slot_old = owner_table(old_place)
    source_slot = jnp.sum(
        jnp.where(new_place[:, None] == jnp.arange(slots)[None, :], slot_old[None, :], 0),
        axis=1,
        dtype=jnp.int32,
    )
    ready = prepare(tokens, norm_gain, w_qkv, lengths, blocks_seen)
    operands = ready + (
        tokens, w_out, moe_gain, w_router, gate_up, w_down, expert_ids, old_place,
    )
    if slots > 4:
        moved = move_by_scatter(gate_up, w_down, source_slot)
        return (layer(*operands)[0],) + moved
    orders = list(itertools.permutations(range(slots)))
    weight = slots ** np.arange(slots)
    codes = jnp.array([int(np.dot(weight, order)) for order in orders], jnp.int32)
    code = jnp.sum(source_slot * jnp.array(weight, jnp.int32))
    index = jnp.sum(jnp.where(codes == code, jnp.arange(len(orders)), 0))

    def branch(order):
        pairs = [(source, slot) for slot, source in enumerate(order)]

        def run(*held):
            rows = [held[7][0, 0].T, held[7][0, 1].T, held[8][0]]
            moving = [lax.ppermute(part, "exp", pairs) for part in rows]
            layer_out, moved = layer(*held, moving=moving)
            return layer_out, jnp.stack([moved[0].T, moved[1].T])[None], moved[2][None]

        return run

    return lax.switch(index, [branch(order) for order in orders], *operands)


def solution(mesh):
    in_specs = (
        P("seq", None),
        P(),
        P(None, None, "exp"),
        P("exp", None),
        P(),
        P(),
        P("exp", None, None, "seq"),
        P("exp", "seq", None),
        P(),
        P("seq", None),
        P(("seq", "exp"), None),
        P(),
        P(),
    )
    out_specs = (P(("seq", "exp"), None), P("exp", None, None, "seq"), P("exp", "seq", None))
    return jax.shard_map(shards, mesh=mesh, in_specs=in_specs, out_specs=out_specs, check_vma=False)
```

```python
import itertools

import jax
import jax.numpy as jnp
import numpy as np
from jax import lax
from jax.sharding import PartitionSpec as P

HEAD_DIM = 64


epsilon = 1e-05
masked_score = -1e30


def rms_scale(values_in, gain):
    widened = values_in.astype(jnp.float32)
    inverse = lax.rsqrt(jnp.mean(widened * widened, axis=-1, keepdims=True) + epsilon)
    return widened * inverse * gain.astype(jnp.float32)


def rotation(angle_base):
    halfway = HEAD_DIM // 2
    spacing = jnp.arange(halfway, dtype=jnp.float32) / halfway
    freqs_all = jnp.exp(-jnp.log(10000.0) * spacing)
    angles = angle_base[:, None] * freqs_all[None, :]
    return jnp.cos(angles), jnp.sin(angles)


def rotate(vectors, cosine, sine_part):
    halfway = vectors.shape[-1] // 2
    cosine = cosine[:, None, :]
    sine_part = sine_part[:, None, :]
    leading = vectors[..., :halfway]
    trailing = vectors[..., halfway:]
    return jnp.concatenate(
        [leading * cosine - trailing * sine_part, trailing * cosine + leading * sine_part], axis=-1
    )


def doc_layout(seq_lengths, row_ids):
    ending = jnp.cumsum(seq_lengths, dtype=jnp.int32)
    passed = (ending[None, :] <= row_ids[:, None]).astype(jnp.int32)
    doc_ids = jnp.sum(passed, axis=1, dtype=jnp.int32)
    starting = jnp.sum(passed * seq_lengths[None, :], axis=1, dtype=jnp.int32)
    return (doc_ids, row_ids - starting)


def owner_table(placing):
    slot_range = jnp.arange(placing.shape[0], dtype=jnp.int32)
    return jnp.sum(
        jnp.where(placing[:, None] == slot_range[None, :], slot_range[:, None], 0),
        axis=0,
        dtype=jnp.int32,
    )


def attend(queries, key_all, value_all, allowed):
    score_scale = queries.shape[-1] ** (-0.5)
    scores = (
        jnp.einsum("qhd,khd->hqk", queries, key_all, preferred_element_type=jnp.float32)
        * score_scale
    )
    scores = jnp.where(allowed[None], scores, masked_score)
    largest = jnp.max(scores, axis=2, keepdims=True)
    weights = jnp.where(allowed[None], jnp.exp(scores - largest), 0.0)
    totals = jnp.sum(weights, axis=2)
    summed = jnp.einsum(
        "hqk,khd->hqd",
        weights.astype(jnp.bfloat16),
        value_all,
        preferred_element_type=jnp.float32,
    )
    return (summed / totals[:, :, None]).astype(jnp.bfloat16)


def from_xor(value, distance):
    count = lax.axis_size("seq")
    return lax.ppermute(value, "seq", [(i, i ^ distance) for i in range(count)])


def gather_xor(value):
    count = lax.axis_size("seq")
    even = [value] + [from_xor(value, k) for k in range(2, count, 2)]
    even = jnp.stack(even)
    odd = from_xor(even, 1)
    return jnp.stack([even, odd], axis=1).reshape((count,) + value.shape)


def reduce_xor(parts):
    count = lax.axis_size("seq")
    pairs = parts.reshape((count // 2, 2) + parts.shape[1:])
    got = from_xor(pairs[:, 1], 1)
    both = pairs[:, 0].astype(jnp.float32) + got.astype(jnp.float32)
    total = both[0]
    sent = both[1:].astype(jnp.bfloat16)
    for k in range(1, count // 2):
        total = total + from_xor(sent[k - 1], 2 * k).astype(jnp.float32)
    return total


def move_by_scatter(gate_up, w_down, source_slot):
    exp_count = lax.axis_size("exp")
    model_width, slice_width = gate_up.shape[2:]
    piece_width = model_width // exp_count
    gate_split = gate_up.reshape(2, exp_count, piece_width, slice_width)
    down_split = w_down.reshape(slice_width, exp_count, piece_width)
    gate_held = lax.all_to_all(gate_split, "exp", split_axis=1, concat_axis=1, tiled=True)
    down_held = lax.all_to_all(down_split, "exp", split_axis=1, concat_axis=1, tiled=True)
    gate_sorted = jnp.take(gate_held, source_slot, axis=1)
    down_sorted = jnp.take(down_held, source_slot, axis=1)
    gate_moved = lax.all_to_all(gate_sorted, "exp", split_axis=1, concat_axis=1, tiled=True)
    down_moved = lax.all_to_all(down_sorted, "exp", split_axis=1, concat_axis=1, tiled=True)
    return gate_moved.reshape(gate_up.shape), down_moved.reshape(w_down.shape)


def prepare(tokens, norm_gain, w_qkv, lengths, blocks_seen):
    block_rows = tokens.shape[0]
    heads_here = w_qkv.shape[2] // HEAD_DIM
    seq_count = lax.axis_size("seq")
    block_index = lax.axis_index("seq")
    query_rows = block_index * block_rows + jnp.arange(block_rows, dtype=jnp.int32)
    query_docs, query_places = doc_layout(lengths, query_rows)
    cosine, sine_part = rotation(query_places.astype(jnp.float32))
    order = block_index ^ jnp.arange(seq_count, dtype=jnp.int32)
    key_rows = (
        order[:, None] * block_rows + jnp.arange(block_rows, dtype=jnp.int32)[None, :]
    ).reshape(-1)
    key_docs, _ = doc_layout(lengths, key_rows)
    seen = jnp.take(blocks_seen[0], order)
    key_seen = jnp.repeat(seen, block_rows) == 1
    allowed = (
        (query_docs[:, None] == key_docs[None, :])
        & (key_rows[None, :] <= query_rows[:, None])
        & key_seen[None, :]
    )
    normed = rms_scale(tokens, norm_gain).astype(jnp.bfloat16)
    projected = [
        lax.optimization_barrier(
            jnp.dot(normed, w_qkv[:, part], preferred_element_type=jnp.float32)
        ).reshape(block_rows, heads_here, HEAD_DIM)
        for part in range(3)
    ]
    queries = rotate(projected[0], cosine, sine_part).astype(jnp.bfloat16)
    key_block = rotate(projected[1], cosine, sine_part).astype(jnp.bfloat16)
    value_block = projected[2].astype(jnp.bfloat16)
    pair = jnp.concatenate(
        [key_block.reshape(block_rows, -1), value_block.reshape(block_rows, -1)], axis=1
    )
    return queries, pair, allowed


def layer(
    queries,
    pair,
    allowed,
    tokens,
    w_out,
    moe_gain,
    w_router,
    gate_up,
    w_down,
    expert_ids,
    old_place,
    moving=(),
):
    block_rows = tokens.shape[0]
    model_width = tokens.shape[1]
    exp_count = lax.axis_size("exp")
    moving = list(moving)
    seq_count = lax.axis_size("seq")
    slot_index = lax.axis_index("exp")
    expert_range = jnp.arange(w_router.shape[1], dtype=jnp.int32)
    heads_here = queries.shape[1]
    pair_all = gather_xor(pair)
    if moving:
        pair_all, moving[0] = lax.optimization_barrier((pair_all, moving[0]))
    pair_all = pair_all.reshape(seq_count * block_rows, 2, heads_here, HEAD_DIM)
    attended = attend(queries, pair_all[:, 0], pair_all[:, 1], allowed)
    attended = jnp.transpose(attended, (1, 0, 2)).reshape(block_rows, heads_here * HEAD_DIM)
    shard_rows = block_rows // exp_count
    partial = jnp.dot(attended, w_out, preferred_element_type=jnp.float32).astype(jnp.bfloat16)
    if moving:
        partial, moving[1] = lax.optimization_barrier((partial, moving[1]))
    partials = lax.all_to_all(
        partial.reshape(exp_count, shard_rows, model_width), "exp", 0, 0, tiled=True
    )
    head_total = jnp.sum(partials.astype(jnp.float32), axis=0)
    residual = lax.dynamic_slice_in_dim(tokens, slot_index * shard_rows, shard_rows, 0)
    hidden = (residual.astype(jnp.float32) + head_total).astype(jnp.bfloat16)
    moe_in = rms_scale(hidden, moe_gain).astype(jnp.bfloat16)
    named = jnp.pad(expert_ids.astype(jnp.bfloat16), ((0, 0), (0, 126)))
    labelled = jnp.concatenate([moe_in, named], axis=1)
    spread = jnp.broadcast_to(labelled[None], (exp_count,) + labelled.shape)
    block_in = lax.all_to_all(spread, "exp", 0, 0, tiled=True).reshape(block_rows, -1)
    all_rows = gather_xor(block_in).reshape(seq_count * block_rows, -1)
    if moving:
        all_rows, moving[2] = lax.optimization_barrier((all_rows, moving[2]))
    flat_rows = all_rows[:, :model_width]
    ids = all_rows[:, model_width : model_width + 2].astype(jnp.int32)
    logits = jnp.dot(flat_rows, w_router, preferred_element_type=jnp.float32)
    chosen = jnp.sum(
        jnp.where(ids[:, :, None] == expert_range[None, None, :], logits[:, None, :], 0.0),
        axis=2,
    )
    gate_first = 1.0 / (1.0 + jnp.exp(chosen[:, 1] - chosen[:, 0]))
    gate_second = 1.0 / (1.0 + jnp.exp(chosen[:, 0] - chosen[:, 1]))
    here = jnp.sum(jnp.where(expert_range == slot_index, old_place, 0))
    gating = jnp.where(
        ids[:, 0] == here, gate_first, jnp.where(ids[:, 1] == here, gate_second, 0.0)
    )
    projected_gate = jnp.dot(flat_rows, gate_up[0, 0], preferred_element_type=jnp.float32)
    projected_up = jnp.dot(flat_rows, gate_up[0, 1], preferred_element_type=jnp.float32)
    activated = (jax.nn.silu(projected_gate) * projected_up).astype(jnp.bfloat16)
    flat_out = jnp.dot(activated, w_down[0], preferred_element_type=jnp.float32)
    weighted = (flat_out * gating[:, None]).astype(jnp.bfloat16)
    summed = reduce_xor(weighted.reshape(seq_count, block_rows, model_width))
    if moving:
        summed, moving[3] = lax.optimization_barrier((summed, moving[3]))
    returned = lax.all_to_all(
        summed.astype(jnp.bfloat16).reshape(exp_count, shard_rows, model_width),
        "exp",
        0,
        0,
        tiled=True,
    )
    moe_sum = jnp.sum(returned.astype(jnp.float32), axis=0)
    layer_out = (hidden.astype(jnp.float32) + moe_sum).astype(jnp.bfloat16)
    return layer_out, moving


def shards(
    tokens,
    norm_gain,
    w_qkv,
    w_out,
    moe_gain,
    w_router,
    gate_up,
    w_down,
    lengths,
    blocks_seen,
    expert_ids,
    old_place,
    new_place,
):
    slots = lax.axis_size("exp")
    slot_old = owner_table(old_place)
    source_slot = jnp.sum(
        jnp.where(new_place[:, None] == jnp.arange(slots)[None, :], slot_old[None, :], 0),
        axis=1,
        dtype=jnp.int32,
    )
    ready = prepare(tokens, norm_gain, w_qkv, lengths, blocks_seen)
    operands = ready + (
        tokens, w_out, moe_gain, w_router, gate_up, w_down, expert_ids, old_place,
    )
    if slots > 4:
        moved = move_by_scatter(gate_up, w_down, source_slot)
        return (layer(*operands)[0],) + moved
    orders = list(itertools.permutations(range(slots)))
    weight = slots ** np.arange(slots)
    codes = jnp.array([int(np.dot(weight, order)) for order in orders], jnp.int32)
    code = jnp.sum(source_slot * jnp.array(weight, jnp.int32))
    index = jnp.sum(jnp.where(codes == code, jnp.arange(len(orders)), 0))

    def branch(order):
        pairs = [(source, slot) for slot, source in enumerate(order)]

        def run(*held):
            gate_rows, up_rows, down_rows = held[7][0, 0].T, held[7][0, 1].T, held[8][0]
            half = down_rows.shape[0] // 2
            parts = [down_rows[:half], down_rows[half:], gate_rows, up_rows]
            moving = [lax.ppermute(part, "exp", pairs) for part in parts]
            layer_out, moved = layer(*held, moving=moving)
            new_down = jnp.concatenate(moved[:2])[None]
            return layer_out, jnp.stack([moved[2].T, moved[3].T])[None], new_down

        return run

    return lax.switch(index, [branch(order) for order in orders], *operands)


def solution(mesh):
    in_specs = (
        P("seq", None),
        P(),
        P(None, None, "exp"),
        P("exp", None),
        P(),
        P(),
        P("exp", None, None, "seq"),
        P("exp", "seq", None),
        P(),
        P("seq", None),
        P(("seq", "exp"), None),
        P(),
        P(),
    )
    out_specs = (P(("seq", "exp"), None), P("exp", None, None, "seq"), P("exp", "seq", None))
    return jax.shard_map(shards, mesh=mesh, in_specs=in_specs, out_specs=out_specs, check_vma=False)
```
